512 devices in a mesh: rows: 16 (over z), vocab: 32 (over x, y, core).
Axes of the slice: x: 4, y: 4, z: 16, core: 2. Of those that a mesh axis runs over, the one named last changes fastest.
Arguments:
- hidden_held: bfloat16 [32, 1, 128, 8192], P('vocab', None, None, 'rows'), may hold values from -64 to 64, as said below
- head_weight: bfloat16 [8192, 131072], P('rows', 'vocab'), may hold values from -0.44194174 to 0.44194174
- state_table: int32 [24, 4096], P(None, 'vocab'), may hold values from -2147483648 to 2147483646
- row_states: int32 [1, 128], P(None, 'rows'), may hold values from 0 to 23
- owner: int32 [1], replicated, may hold values from 0 to 31
Outputs:
- log_probs: float32 [1, 128, 131072], P(None, 'rows', 'vocab')
- entropy: float32 [1, 128], P(None, 'rows')
The draws below stay inside these ranges and needn't reach their ends.
Inputs may be any that keep to these rules, and one draw needn't show every extreme that they name: `hidden_held`: rows of a holder that owner does not name are not read.
All inputs are finite; a program needn't handle non-finite values.
Results may differ from the reference program's by a relative error of at most 0.0003.
Values may be sent and summed in bfloat16 or wider, within the bound.
No kernel may reach another device: no remote copies, remote signals or barrier semaphores. Data moves between devices by JAX's collectives and lax.ppermute only.
A program may use at most 64 MiB of HBM per device.

```python
import math
import jax
import jax.numpy as jnp
from jax import lax

D = 8192
STATES = 24
MBR = 128
MICRO = 1
V = 131072
WORDS = 4096
HOLDERS = 32
SLAB = 512
N_ROWS = 16


def column_draw(key, column):
    values = jax.random.normal(jax.random.fold_in(jax.random.fold_in(key, 11), column), (D,), jnp.float32)
    spread = jax.random.uniform(jax.random.fold_in(jax.random.fold_in(key, 12), column), (), jnp.float32, math.log(0.75), math.log(7.5))
    factor = jnp.exp(spread)
    return (jnp.clip(values, -5.0, 5.0) * factor / math.sqrt(D), factor)


def draw_head_weight(key, part):
    columns, factors = jax.vmap(lambda column: column_draw(key, column))(jnp.arange(V, dtype=jnp.int32))
    return columns.T.astype(jnp.bfloat16)


def draw_hidden_held(key, part):
    shape_full = (HOLDERS, MICRO, MBR, D)
    spread = jax.random.uniform(jax.random.fold_in(key, 13), (HOLDERS, MICRO, MBR, 1), jnp.float32, math.log(0.4), math.log(4.0))
    base = jnp.clip(jax.random.normal(jax.random.fold_in(key, 14), shape_full, jnp.float32), -5.0, 5.0)
    result = base * jnp.exp(spread)
    return jnp.clip(result, -64.0, 64.0).astype(jnp.bfloat16)


def place_ends(values, stream_key, least, top_value):
    longest = values.shape.index(max(values.shape))
    spots = []
    for shift in (0, 1):
        where = [jax.random.randint(jax.random.fold_in(stream_key, axis), (), 0, length) for axis, length in enumerate(values.shape)]
        where[longest] = (where[longest] + shift) % values.shape[longest]
        spots.append(tuple(where))
    return values.at[spots[0]].set(least).at[spots[1]].set(top_value)


def setup_inputs(seed: int = 0) -> dict:
    seeds = jax.random.split(jax.random.key(seed), 6)
    hidden_held = draw_hidden_held(jax.random.fold_in(seeds[5], 71), 0)
    head_weight = draw_head_weight(jax.random.fold_in(seeds[5], 71), 0)
    state_table = place_ends(jax.random.randint(seeds[2], (STATES, WORDS), -2147483648, 2147483647), jax.random.fold_in(seeds[2], 1), -2147483648, 2147483646).astype(jnp.int32)
    row_states = place_ends(jax.random.randint(seeds[3], (MICRO, MBR), 0, STATES), jax.random.fold_in(seeds[3], 1), 0, STATES - 1).astype(jnp.int32)
    owner = jax.random.randint(seeds[4], (MICRO,), 0, HOLDERS).astype(jnp.int32)
    return dict(hidden_held=hidden_held, head_weight=head_weight, state_table=state_table, row_states=row_states, owner=owner)


def unpack_table(state_table):
    bit_shifts = jnp.arange(32, dtype=jnp.int32)
    flags = jnp.bitwise_and(jnp.right_shift(state_table[:, :, None], bit_shifts), 1)
    return flags.reshape(state_table.shape[0], -1)


def reference(hidden_held, head_weight, state_table, row_states, owner):
    allowed_table = unpack_table(state_table).astype(jnp.float32)
    batch_rows = hidden_held[owner, jnp.arange(MICRO)]

    def one_batch(inputs):
        rows_here, states_here = inputs

        def add_block(block, running):
            start = (block * SLAB).astype(jnp.int32)
            left_part = lax.dynamic_slice_in_dim(rows_here, start, SLAB, 1)
            right_part = lax.dynamic_slice_in_dim(head_weight, start, SLAB, 0)
            partial_value = jnp.dot(left_part, right_part, preferred_element_type=jnp.float32)
            return running + partial_value

        logits = lax.fori_loop(0, N_ROWS, add_block, jnp.zeros((MBR, V), jnp.float32))
        allowed = allowed_table[states_here] > 0.5
        masked = jnp.where(allowed, logits, jnp.float32(-1e30))
        row_max = jnp.max(masked, axis=1)
        scaled = jnp.where(allowed, jnp.exp(logits - row_max[:, None]), jnp.float32(0.0))
        total = jnp.sum(scaled, axis=1)
        weighted = jnp.sum(jnp.where(allowed, scaled * logits, jnp.float32(0.0)), axis=1)
        log_norm = row_max + jnp.log(total)
        log_probs = jnp.where(allowed, logits - log_norm[:, None], jnp.float32(0.0))
        entropy = log_norm - weighted / total
        return log_probs, entropy

    log_probs, entropy = lax.map(one_batch, (batch_rows, row_states))
    return log_probs, entropy
```

```python
import jax
import jax.numpy as jnp
from jax import lax
from jax.experimental import pallas as pl
from jax.experimental.pallas import tpu as pltpu
from jax.sharding import PartitionSpec as P

N = 4096
HALF = N // 2
TAIL = 128
TILES = 8
WIDE = N // TILES
F32 = jnp.float32
I16 = jnp.int16


def encode(values):
    top = jnp.max(jnp.abs(values), axis=1, keepdims=True)
    k = jnp.ceil(8.0 * jnp.log2(jnp.maximum(top, 1e-30) * (1.0 / 32000.0)))
    return jnp.round(values * jnp.exp2(-0.125 * k)), k


def to_i16(values):
    return values.astype(jnp.int32).astype(I16)


def to_f32(codes):
    return codes.astype(jnp.int32).astype(F32)


def scale_of(codes):
    return jnp.exp2(0.125 * to_f32(codes)[:, :1])


def product_kernel(z_ref, x_ref, w_ref, own_ref, up_ref, down_ref, up2_ref, down2_ref, xp_ref, acc_ref):
    step = pl.program_id(0)

    @pl.when(step == 0)
    def _():
        x = jnp.concatenate([x_ref[8 * c : 8 * c + 8].reshape(128, 128) for c in range(4)], axis=1)
        i = lax.broadcasted_iota(jnp.int32, (128, 128), 0)
        source = lax.broadcasted_iota(jnp.int32, (128, 128), 1)
        b = i >> 5
        piece = (z_ref[0] + jnp.where(b == 3, -1, b) + 4 * ((i >> 3) & 3)) & 15
        chosen = (source == 8 * piece + (i & 7)).astype(F32).astype(jnp.bfloat16)
        xp_ref[...] = jnp.dot(chosen, x, preferred_element_type=F32).astype(jnp.bfloat16)

    acc_ref[step] = jnp.dot(xp_ref[...], w_ref[...], preferred_element_type=F32)

    @pl.when(step == TILES - 1)
    def _():
        def rows(lo, hi):
            return jnp.concatenate([acc_ref[t, lo:hi, :] for t in range(TILES)], axis=1)

        own_ref[...] = rows(0, 32)
        for ref, lo in ((up_ref, 32), (down_ref, 96)):
            q, k = encode(rows(lo, lo + 32))
            ref[:, :N] = to_i16(q)
            ref[:, N:] = to_i16(jnp.broadcast_to(k, (32, TAIL)))
        q, k = encode(rows(64, 96))
        tail = to_i16(jnp.broadcast_to(k, (32, TAIL)))
        up2_ref[:, :HALF] = to_i16(q[:, :HALF])
        up2_ref[:, HALF:] = tail
        down2_ref[:, :HALF] = to_i16(q[:, HALF:])
        down2_ref[:, HALF:] = tail


def product(z, x, w):
    def full(shape):
        return pl.BlockSpec(shape, lambda t: (0,) * len(shape))

    outs = ((32, N), (32, N + TAIL), (32, N + TAIL), (32, HALF + TAIL), (32, HALF + TAIL))
    return pl.pallas_call(
        product_kernel,
        grid=(TILES,),
        in_specs=[
            pl.BlockSpec(memory_space=pltpu.SMEM),
            full(x.shape),
            pl.BlockSpec((w.shape[0], WIDE), lambda t: (0, t)),
        ],
        out_specs=[full(s) for s in outs],
        out_shape=[jax.ShapeDtypeStruct(s, F32 if n == 0 else I16) for n, s in enumerate(outs)],
        scratch_shapes=[
            pltpu.VMEM((128, w.shape[0]), jnp.bfloat16),
            pltpu.VMEM((TILES, 128, WIDE), F32),
        ],
        compiler_params=pltpu.CompilerParams(vmem_limit_bytes=24 * 2**20),
        cost_estimate=pl.CostEstimate(flops=2 * 128 * 512 * N, bytes_accessed=6 * 2**20, transcendentals=0),
    )(z, x, w)


def first_sum_kernel(own_ref, low_ref, high_ref, low2_ref, high2_ref, keep_ref, up_ref, far_ref, down_ref):
    near = (
        own_ref[...]
        + to_f32(low_ref[:, :N]) * scale_of(low_ref[:, N:])
        + to_f32(high_ref[:, :N]) * scale_of(high_ref[:, N:])
    )
    left = to_f32(low2_ref[:, :HALF]) * scale_of(low2_ref[:, HALF:])
    right = to_f32(high2_ref[:, :HALF]) * scale_of(high2_ref[:, HALF:])
    right = jnp.concatenate([right[24:], right[:24]], axis=0)
    total = near + jnp.concatenate([left, right], axis=1)
    keep_ref[...] = total[:8]
    for ref, lo in ((up_ref, 8), (far_ref, 16), (down_ref, 24)):
        q, k = encode(total[lo : lo + 8])
        ref[:, :HALF] = to_i16(jnp.concatenate([q[:, :HALF], q[:, HALF:]], axis=0))
        ref[:, HALF:] = to_i16(jnp.broadcast_to(jnp.concatenate([k, k], axis=0), (16, TAIL)))


def first_sum(*arrays):
    coded = jax.ShapeDtypeStruct((16, HALF + TAIL), I16)
    return pl.pallas_call(
        first_sum_kernel,
        out_shape=[jax.ShapeDtypeStruct((8, N), F32), coded, coded, coded],
        compiler_params=pltpu.CompilerParams(vmem_limit_bytes=24 * 2**20),
        cost_estimate=pl.CostEstimate(flops=2**20, bytes_accessed=2 * 2**20, transcendentals=0),
    )(*arrays)


def stats_kernel(own_ref, a_ref, b_ref, c_ref, allowed_ref, logits_ref, stats_ref):
    logits = own_ref[...]
    for ref in (a_ref, b_ref, c_ref):
        part = to_f32(ref[:, :HALF]) * scale_of(ref[:, HALF:])
        logits = logits + jnp.concatenate([part[:8], part[8:]], axis=1)
    logits_ref[...] = logits
    allowed = allowed_ref[...] > 0.5
    top = jnp.max(jnp.where(allowed, logits, -1e30), axis=1, keepdims=True)
    scaled = jnp.where(allowed, jnp.exp(logits - top), 0.0)
    total = jnp.sum(scaled, axis=1, keepdims=True)
    weighted = jnp.sum(jnp.where(allowed, scaled * logits, 0.0), axis=1, keepdims=True)
    lane = lax.broadcasted_iota(jnp.int32, (8, 128), 1)
    tile = jnp.where(lane == 0, top, jnp.where(lane == 1, total, jnp.where(lane == 2, weighted, 0.0)))
    stats_ref[...] = jnp.broadcast_to(tile[None], stats_ref.shape)


def finish_kernel(logits_ref, allowed_ref, stats_ref, log_probs_ref, entropy_ref):
    stats = stats_ref[...]
    top = stats[:, :, 0:1]
    row_max = jnp.max(top, axis=0)
    factor = jnp.exp(top - row_max[None])
    total = jnp.sum(stats[:, :, 1:2] * factor, axis=0)
    weighted = jnp.sum(stats[:, :, 2:3] * factor, axis=0)
    log_norm = row_max + jnp.log(total)
    log_probs_ref[...] = jnp.where(allowed_ref[...] > 0.5, logits_ref[...] - log_norm, 0.0)
    entropy_ref[...] = jnp.broadcast_to(log_norm - weighted / total, entropy_ref.shape)


def spread(array, axis):
    return lax.all_to_all(array, axis, 0, 0)


def shift(array, step):
    count = lax.axis_size("rows")
    return lax.ppermute(array, "rows", [(i, (i + step) % count) for i in range(count)])


def shards(hidden_held, head_weight, state_table, row_states, owner):
    z = lax.axis_index("rows").astype(jnp.int32)[None]
    chunks = hidden_held[0, 0].reshape(8, 16, 4, 128).transpose(2, 0, 1, 3).reshape(32, 16, 128)
    mine = lax.dynamic_index_in_dim(spread(chunks, "vocab"), owner[0], 0, keepdims=True)
    x = spread(jnp.broadcast_to(mine, (32, 16, 128)), "vocab")

    own, up, down, up2, down2 = product(z, x, head_weight)
    own, up, far, down = first_sum(own, shift(up, 1), shift(down, -1), shift(up2, 2), shift(down2, -2))

    words = state_table[row_states[0]]
    bits = jnp.right_shift(words[:, :, None], jnp.arange(32, dtype=jnp.int32)) & 1
    allowed = bits.astype(F32).reshape(8, N)

    parts = (shift(up, 4), shift(far, 8), shift(down, -4))
    logits, stats = pl.pallas_call(
        stats_kernel,
        out_shape=[jax.ShapeDtypeStruct((8, N), F32), jax.ShapeDtypeStruct((32, 8, 128), F32)],
    )(own, *parts, allowed)
    stats = spread(stats, "vocab")
    log_probs, entropy = pl.pallas_call(
        finish_kernel,
        out_shape=[jax.ShapeDtypeStruct((8, N), F32), jax.ShapeDtypeStruct((8, 128), F32)],
    )(logits, allowed, stats)
    return log_probs[None], entropy[:, 0][None]


def solution(mesh):
    return jax.shard_map(
        shards,
        mesh=mesh,
        in_specs=(
            P("vocab", None, None, "rows"),
            P("rows", "vocab"),
            P(None, "vocab"),
            P(None, "rows"),
            P(),
        ),
        out_specs=(P(None, "rows", "vocab"), P(None, "rows")),
        check_vma=False,
    )
```

```python
import jax
import jax.numpy as jnp
from jax import lax
from jax.experimental import pallas as pl
from jax.experimental.pallas import tpu as pltpu
from jax.sharding import PartitionSpec as P

N = 4096
HALF = N // 2
TAIL = 128
TILES = 8
WIDE = N // TILES
F32 = jnp.float32
I16 = jnp.int16


def encode(values):
    top = jnp.max(jnp.abs(values), axis=1, keepdims=True)
    k = jnp.ceil(8.0 * jnp.log2(jnp.maximum(top, 1e-30) * (1.0 / 32000.0)))
    return jnp.round(values * jnp.exp2(-0.125 * k)), k


def to_i16(values):
    return values.astype(jnp.int32).astype(I16)


def to_f32(codes):
    return codes.astype(jnp.int32).astype(F32)


def scale_of(codes):
    return jnp.exp2(0.125 * to_f32(codes)[:, :1])


def product_kernel(z_ref, x_ref, w_ref, own_ref, up_ref, down_ref, up2_ref, down2_ref, acc_ref, held_ref, sems):
    def tile(t):
        part = pl.ds(t * WIDE, WIDE)
        return pltpu.make_async_copy(w_ref.at[:, part], held_ref.at[:, part], sems.at[t])

    for t in range(TILES):
        tile(t).start()
    x = x_ref[...].astype(F32).reshape(16, 2, 2, 8, 128)
    x = [x[:, h, t].reshape(128, 128) for h in range(2) for t in range(2)]
    x = jnp.concatenate(x, axis=1).astype(jnp.bfloat16)
    i = lax.broadcasted_iota(jnp.int32, (128, 128), 0)
    source = lax.broadcasted_iota(jnp.int32, (128, 128), 1)
    b = i >> 5
    piece = (z_ref[0] + jnp.where(b == 3, -1, b) + 4 * ((i >> 3) & 3)) & 15
    chosen = (source == 8 * piece + (i & 7)).astype(F32).astype(jnp.bfloat16)
    x = jnp.dot(chosen, x, preferred_element_type=F32).astype(jnp.bfloat16)
    for t in range(TILES):
        tile(t).wait()
        acc_ref[:, t * WIDE : (t + 1) * WIDE] = jnp.dot(
            x, held_ref[:, t * WIDE : (t + 1) * WIDE], preferred_element_type=F32
        )
    own_ref[...] = acc_ref[:32]
    for ref, lo in ((up_ref, 32), (down_ref, 96)):
        q, k = encode(acc_ref[lo : lo + 32])
        ref[:, :N] = to_i16(q)
        ref[:, N:] = to_i16(jnp.broadcast_to(k, (32, TAIL)))
    q, k = encode(acc_ref[64:96])
    tail = to_i16(jnp.broadcast_to(k, (32, TAIL)))
    up2_ref[:, :HALF] = to_i16(q[:, :HALF])
    up2_ref[:, HALF:] = tail
    down2_ref[:, :HALF] = to_i16(q[:, HALF:])
    down2_ref[:, HALF:] = tail


def product(z, x, w):
    outs = ((32, N), (32, N + TAIL), (32, N + TAIL), (32, HALF + TAIL), (32, HALF + TAIL))
    return pl.pallas_call(
        product_kernel,
        in_specs=[
            pl.BlockSpec(memory_space=pltpu.SMEM),
            pl.BlockSpec(memory_space=pltpu.VMEM),
            pl.BlockSpec(memory_space=pl.ANY),
        ],
        out_shape=[jax.ShapeDtypeStruct(s, F32 if n == 0 else I16) for n, s in enumerate(outs)],
        scratch_shapes=[
            pltpu.VMEM((128, N), F32),
            pltpu.VMEM(w.shape, w.dtype),
            pltpu.SemaphoreType.DMA((TILES,)),
        ],
        compiler_params=pltpu.CompilerParams(vmem_limit_bytes=50 * 2**20),
        cost_estimate=pl.CostEstimate(flops=2 * 128 * 512 * N, bytes_accessed=6 * 2**20, transcendentals=0),
    )(z, x, w)


def first_sum_kernel(own_ref, low_ref, high_ref, low2_ref, high2_ref, keep_ref, up_ref, far_ref, down_ref):
    near = (
        own_ref[...]
        + to_f32(low_ref[:, :N]) * scale_of(low_ref[:, N:])
        + to_f32(high_ref[:, :N]) * scale_of(high_ref[:, N:])
    )
    left = to_f32(low2_ref[:, :HALF]) * scale_of(low2_ref[:, HALF:])
    right = to_f32(high2_ref[:, :HALF]) * scale_of(high2_ref[:, HALF:])
    right = jnp.concatenate([right[24:], right[:24]], axis=0)
    total = near + jnp.concatenate([left, right], axis=1)
    keep_ref[...] = total[:8]
    for ref, lo in ((up_ref, 8), (far_ref, 16), (down_ref, 24)):
        q, k = encode(total[lo : lo + 8])
        ref[:, :HALF] = to_i16(jnp.concatenate([q[:, :HALF], q[:, HALF:]], axis=0))
        ref[:, HALF:] = to_i16(jnp.broadcast_to(jnp.concatenate([k, k], axis=0), (16, TAIL)))


def first_sum(*arrays):
    coded = jax.ShapeDtypeStruct((16, HALF + TAIL), I16)
    return pl.pallas_call(
        first_sum_kernel,
        out_shape=[jax.ShapeDtypeStruct((8, N), F32), coded, coded, coded],
        compiler_params=pltpu.CompilerParams(vmem_limit_bytes=24 * 2**20),
        cost_estimate=pl.CostEstimate(flops=2**20, bytes_accessed=2 * 2**20, transcendentals=0),
    )(*arrays)


def stats_kernel(own_ref, a_ref, b_ref, c_ref, allowed_ref, logits_ref, stats_ref):
    logits = own_ref[...]
    for ref in (a_ref, b_ref, c_ref):
        part = to_f32(ref[:, :HALF]) * scale_of(ref[:, HALF:])
        logits = logits + jnp.concatenate([part[:8], part[8:]], axis=1)
    logits_ref[...] = logits
    allowed = allowed_ref[...] > 0.5
    top = jnp.max(jnp.where(allowed, logits, -1e30), axis=1, keepdims=True)
    scaled = jnp.where(allowed, jnp.exp(logits - top), 0.0)
    total = jnp.sum(scaled, axis=1, keepdims=True)
    weighted = jnp.sum(jnp.where(allowed, scaled * logits, 0.0), axis=1, keepdims=True)
    own_lane = lax.broadcasted_iota(jnp.int32, (8, 128), 1) == lax.broadcasted_iota(jnp.int32, (8, 128), 0)
    for n, column in enumerate((top, total, weighted)):
        row = jnp.sum(jnp.where(own_lane, column, 0.0), axis=0, keepdims=True)
        stats_ref[:, :, 128 * n : 128 * n + 128] = jnp.broadcast_to(row[None], (32, 1, 128))


def finish_kernel(logits_ref, allowed_ref, stats_ref, log_probs_ref, entropy_ref):
    top = stats_ref[:, :, :128]
    row_max = jnp.max(top, axis=0)
    factor = jnp.exp(top - row_max[None])
    lane = lax.broadcasted_iota(jnp.int32, (1, 128), 1)
    total = jnp.where(lane < 8, jnp.sum(stats_ref[:, :, 128:256] * factor, axis=0), 1.0)
    weighted = jnp.sum(stats_ref[:, :, 256:] * factor, axis=0)
    log_norm = row_max + jnp.log(total)
    entropy_ref[...] = (log_norm - weighted / total)[:, :8]
    own_lane = lax.broadcasted_iota(jnp.int32, (8, 128), 1) == lax.broadcasted_iota(jnp.int32, (8, 128), 0)
    column = jnp.sum(jnp.where(own_lane, log_norm, 0.0), axis=1, keepdims=True)
    log_probs_ref[0] = jnp.where(allowed_ref[...] > 0.5, logits_ref[...] - column, 0.0)


def spread(array, axis):
    return lax.all_to_all(array, axis, 0, 0)


def shift(array, step):
    count = lax.axis_size("rows")
    return lax.ppermute(array, "rows", [(i, (i + step) % count) for i in range(count)])


def shards(hidden_held, head_weight, state_table, row_states, owner):
    z = lax.axis_index("rows").astype(jnp.int32)[None]
    chunks = hidden_held[0, 0].reshape(16, 8, 4, 128).transpose(0, 2, 1, 3).reshape(32, 16, 128)
    mine = lax.dynamic_index_in_dim(spread(chunks, "vocab"), owner[0], 0, keepdims=True)
    x = spread(jnp.broadcast_to(mine, (32, 16, 128)), "vocab")

    own, up, down, up2, down2 = product(z, x, head_weight)
    low2, low, high, high2 = shift(up2, 2), shift(up, 1), shift(down, -1), shift(down2, -2)
    own, up, far, down = first_sum(own, low, high, low2, high2)

    words = state_table[row_states[0]]
    bits = jnp.right_shift(words[:, :, None], jnp.arange(32, dtype=jnp.int32)) & 1
    allowed = bits.astype(F32).reshape(8, N)

    parts = (shift(far, 8), shift(up, 4), shift(down, -4))
    logits, stats = pl.pallas_call(
        stats_kernel,
        out_shape=[jax.ShapeDtypeStruct((8, N), F32), jax.ShapeDtypeStruct((32, 1, 384), F32)],
        compiler_params=pltpu.CompilerParams(vmem_limit_bytes=24 * 2**20),
    )(own, *parts, allowed)
    stats = spread(stats, "vocab")
    return tuple(
        pl.pallas_call(
            finish_kernel,
            out_shape=[jax.ShapeDtypeStruct((1, 8, N), F32), jax.ShapeDtypeStruct((1, 8), F32)],
            compiler_params=pltpu.CompilerParams(vmem_limit_bytes=24 * 2**20),
        )(logits, allowed, stats)
    )


def solution(mesh):
    return jax.shard_map(
        shards,
        mesh=mesh,
        in_specs=(
            P("vocab", None, None, "rows"),
            P("rows", "vocab"),
            P(None, "vocab"),
            P(None, "rows"),
            P(),
        ),
        out_specs=(P(None, "rows", "vocab"), P(None, "rows")),
        check_vma=False,
    )
```

```python
import jax
import jax.numpy as jnp
from jax import lax
from jax.experimental import pallas as pl
from jax.experimental.pallas import tpu as pltpu
from jax.sharding import PartitionSpec as P

N = 4096
HALF = N // 2
TAIL = 128
TILES = 8
WIDE = N // TILES
F32 = jnp.float32
I16 = jnp.int16


def encode(values):
    top = jnp.max(jnp.abs(values), axis=1, keepdims=True)
    k = jnp.ceil(8.0 * jnp.log2(jnp.maximum(top, 1e-30) * (1.0 / 32000.0)))
    return jnp.round(values * jnp.exp2(-0.125 * k)), k


def to_i16(values):
    return values.astype(jnp.int32).astype(I16)


def to_f32(codes):
    return codes.astype(jnp.int32).astype(F32)


def scale_of(codes):
    return jnp.exp2(0.125 * to_f32(codes)[:, :1])


def product_kernel(z_ref, x_ref, w_ref, own_ref, up_ref, up2_ref, down_ref, acc_ref, held_ref, sems):
    def tile(t):
        part = pl.ds(t * WIDE, WIDE)
        return pltpu.make_async_copy(w_ref.at[:, part], held_ref.at[:, part], sems.at[t])

    for t in range(TILES):
        tile(t).start()
    x = x_ref[...].astype(F32).reshape(16, 2, 2, 8, 128)
    x = [x[:, h, t].reshape(128, 128) for h in range(2) for t in range(2)]
    x = jnp.concatenate(x, axis=1).astype(jnp.bfloat16)
    i = lax.broadcasted_iota(jnp.int32, (128, 128), 0)
    source = lax.broadcasted_iota(jnp.int32, (128, 128), 1)
    b = i >> 5
    piece = (z_ref[0] + z_ref[1] * (jnp.where(b == 3, -1, b) + 4 * ((i >> 3) & 3))) & 15
    chosen = (source == 8 * piece + (i & 7)).astype(F32).astype(jnp.bfloat16)
    x = jnp.dot(chosen, x, preferred_element_type=F32).astype(jnp.bfloat16)
    for t in range(TILES):
        tile(t).wait()
        acc_ref[:, t * WIDE : (t + 1) * WIDE] = jnp.dot(
            x, held_ref[:, t * WIDE : (t + 1) * WIDE], preferred_element_type=F32
        )
    own_ref[...] = acc_ref[:32]
    for ref, lo in ((up_ref, 32), (up2_ref, 64), (down_ref, 96)):
        q, k = encode(acc_ref[lo : lo + 32])
        ref[:, :N] = to_i16(q)
        ref[:, N:] = to_i16(jnp.broadcast_to(k, (32, TAIL)))


def product(z, x, w):
    outs = ((32, N), (32, N + TAIL), (32, N + TAIL), (32, N + TAIL))
    return pl.pallas_call(
        product_kernel,
        in_specs=[
            pl.BlockSpec(memory_space=pltpu.SMEM),
            pl.BlockSpec(memory_space=pltpu.VMEM),
            pl.BlockSpec(memory_space=pl.ANY),
        ],
        out_shape=[jax.ShapeDtypeStruct(s, F32 if n == 0 else I16) for n, s in enumerate(outs)],
        scratch_shapes=[
            pltpu.VMEM((128, N), F32),
            pltpu.VMEM(w.shape, w.dtype),
            pltpu.SemaphoreType.DMA((TILES,)),
        ],
        compiler_params=pltpu.CompilerParams(vmem_limit_bytes=50 * 2**20),
        cost_estimate=pl.CostEstimate(flops=2 * 128 * 512 * N, bytes_accessed=6 * 2**20, transcendentals=0),
    )(z, x, w)


def first_sum_kernel(own_ref, a_ref, b_ref, c_ref, keep_ref, up_ref, far_ref, down_ref):
    total = own_ref[...]
    for ref in (a_ref, b_ref, c_ref):
        total = total + to_f32(ref[:, :N]) * scale_of(ref[:, N:])
    keep_ref[...] = total[:8]
    for ref, lo in ((up_ref, 8), (far_ref, 16), (down_ref, 24)):
        q, k = encode(total[lo : lo + 8])
        ref[:, :HALF] = to_i16(jnp.concatenate([q[:, :HALF], q[:, HALF:]], axis=0))
        ref[:, HALF:] = to_i16(jnp.broadcast_to(jnp.concatenate([k, k], axis=0), (16, TAIL)))


def first_sum(*arrays):
    coded = jax.ShapeDtypeStruct((16, HALF + TAIL), I16)
    return pl.pallas_call(
        first_sum_kernel,
        out_shape=[jax.ShapeDtypeStruct((8, N), F32), coded, coded, coded],
        compiler_params=pltpu.CompilerParams(vmem_limit_bytes=24 * 2**20),
        cost_estimate=pl.CostEstimate(flops=2**20, bytes_accessed=2 * 2**20, transcendentals=0),
    )(*arrays)


def stats_kernel(own_ref, a_ref, b_ref, c_ref, allowed_ref, logits_ref, stats_ref):
    logits = own_ref[...]
    for ref in (a_ref, b_ref, c_ref):
        part = to_f32(ref[:, :HALF]) * scale_of(ref[:, HALF:])
        logits = logits + jnp.concatenate([part[:8], part[8:]], axis=1)
    logits_ref[...] = logits
    allowed = allowed_ref[...] > 0.5
    top = jnp.max(jnp.where(allowed, logits, -1e30), axis=1, keepdims=True)
    scaled = jnp.where(allowed, jnp.exp(logits - top), 0.0)
    total = jnp.sum(scaled, axis=1, keepdims=True)
    weighted = jnp.sum(jnp.where(allowed, scaled * logits, 0.0), axis=1, keepdims=True)
    own_lane = lax.broadcasted_iota(jnp.int32, (8, 128), 1) == lax.broadcasted_iota(jnp.int32, (8, 128), 0)
    for n, column in enumerate((top, total, weighted)):
        row = jnp.sum(jnp.where(own_lane, column, 0.0), axis=0, keepdims=True)
        stats_ref[:, :, 128 * n : 128 * n + 128] = jnp.broadcast_to(row[None], (32, 1, 128))


def finish_kernel(logits_ref, allowed_ref, stats_ref, log_probs_ref, entropy_ref):
    top = stats_ref[:, :, :128]
    row_max = jnp.max(top, axis=0)
    factor = jnp.exp(top - row_max[None])
    lane = lax.broadcasted_iota(jnp.int32, (1, 128), 1)
    total = jnp.where(lane < 8, jnp.sum(stats_ref[:, :, 128:256] * factor, axis=0), 1.0)
    weighted = jnp.sum(stats_ref[:, :, 256:] * factor, axis=0)
    log_norm = row_max + jnp.log(total)
    entropy_ref[...] = (log_norm - weighted / total)[:, :8]
    own_lane = lax.broadcasted_iota(jnp.int32, (8, 128), 1) == lax.broadcasted_iota(jnp.int32, (8, 128), 0)
    column = jnp.sum(jnp.where(own_lane, log_norm, 0.0), axis=1, keepdims=True)
    log_probs_ref[0] = jnp.where(allowed_ref[...] > 0.5, logits_ref[...] - column, 0.0)


def spread(array, axis):
    return lax.all_to_all(array, axis, 0, 0)


def shift(array, step):
    rows, columns = lax.axis_size("rows"), lax.axis_size("vocab")
    pairs = [
        (z * columns + v, (z + (step if v % 2 == 0 else -step)) % rows * columns + v)
        for z in range(rows)
        for v in range(columns)
    ]
    return lax.ppermute(array, ("rows", "vocab"), pairs)


def shards(hidden_held, head_weight, state_table, row_states, owner):
    z = jnp.stack([lax.axis_index("rows"), 1 - 2 * (lax.axis_index("vocab") % 2)]).astype(jnp.int32)
    chunks = hidden_held[0, 0].reshape(16, 8, 4, 128).transpose(0, 2, 1, 3).reshape(32, 16, 128)
    mine = lax.dynamic_index_in_dim(spread(chunks, "vocab"), owner[0], 0, keepdims=True)
    x = spread(jnp.broadcast_to(mine, (32, 16, 128)), "vocab")

    own, up, up2, down = product(z, x, head_weight)
    own, up, far, down = first_sum(own, shift(up, 1), shift(up2, 2), shift(down, -1))

    words = state_table[row_states[0]]
    bits = jnp.right_shift(words[:, :, None], jnp.arange(32, dtype=jnp.int32)) & 1
    allowed = bits.astype(F32).reshape(8, N)

    parts = (shift(far, 8), shift(up, 4), shift(down, -4))
    logits, stats = pl.pallas_call(
        stats_kernel,
        out_shape=[jax.ShapeDtypeStruct((8, N), F32), jax.ShapeDtypeStruct((32, 1, 384), F32)],
        compiler_params=pltpu.CompilerParams(vmem_limit_bytes=24 * 2**20),
    )(own, *parts, allowed)
    stats = spread(stats, "vocab")
    return tuple(
        pl.pallas_call(
            finish_kernel,
            out_shape=[jax.ShapeDtypeStruct((1, 8, N), F32), jax.ShapeDtypeStruct((1, 8), F32)],
            compiler_params=pltpu.CompilerParams(vmem_limit_bytes=24 * 2**20),
        )(logits, allowed, stats)
    )


def solution(mesh):
    return jax.shard_map(
        shards,
        mesh=mesh,
        in_specs=(
            P("vocab", None, None, "rows"),
            P("rows", "vocab"),
            P(None, "vocab"),
            P(None, "rows"),
            P(),
        ),
        out_specs=(P(None, "rows", "vocab"), P(None, "rows")),
        check_vma=False,
    )
```

```python
import jax
import jax.numpy as jnp
from jax import lax
from jax.experimental import pallas as pl
from jax.experimental.pallas import tpu as pltpu
from jax.sharding import PartitionSpec as P

N = 4096
HALF = N // 2
TAIL = 128
TILES = 8
WIDE = N // TILES
F32 = jnp.float32
I16 = jnp.int16


def encode(values):
    top = jnp.max(jnp.abs(values), axis=1, keepdims=True)
    k = jnp.ceil(8.0 * jnp.log2(jnp.maximum(top, 1e-30) * (1.0 / 32000.0)))
    return jnp.round(values * jnp.exp2(-0.125 * k)), k


def to_i16(values):
    return values.astype(jnp.int32).astype(I16)


def to_f32(codes):
    return codes.astype(jnp.int32).astype(F32)


def scale_of(codes):
    return jnp.exp2(0.125 * to_f32(codes)[:, :1])


def product_kernel(z_ref, x_ref, w_ref, own_ref, up_ref, up2_ref, down_ref, acc_ref, held_ref, sems):
    def tile(t):
        part = pl.ds(t * WIDE, WIDE)
        return pltpu.make_async_copy(w_ref.at[:, part], held_ref.at[:, part], sems.at[t])

    for t in range(TILES):
        tile(t).start()
    x = x_ref[...].astype(F32).reshape(16, 2, 2, 8, 128)
    x = [x[:, h, t].reshape(128, 128) for h in range(2) for t in range(2)]
    x = jnp.concatenate(x, axis=1).astype(jnp.bfloat16)
    i = lax.broadcasted_iota(jnp.int32, (128, 128), 0)
    source = lax.broadcasted_iota(jnp.int32, (128, 128), 1)
    b = i >> 5
    piece = ((z_ref[0] & 15) + (1 - 2 * (z_ref[0] >> 4)) * (jnp.where(b == 3, -1, b) + 4 * ((i >> 3) & 3))) & 15
    chosen = (source == 8 * piece + (i & 7)).astype(F32).astype(jnp.bfloat16)
    x = jnp.dot(chosen, x, preferred_element_type=F32).astype(jnp.bfloat16)
    for t in range(TILES):
        tile(t).wait()
        acc_ref[:, t * WIDE : (t + 1) * WIDE] = jnp.dot(
            x, held_ref[:, t * WIDE : (t + 1) * WIDE], preferred_element_type=F32
        )
    own_ref[...] = acc_ref[:32]
    for ref, lo in ((up_ref, 32), (up2_ref, 64), (down_ref, 96)):
        q, k = encode(acc_ref[lo : lo + 32])
        ref[:, :N] = to_i16(q)
        ref[:, N:] = to_i16(jnp.broadcast_to(k, (32, TAIL)))


def product(z, x, w):
    outs = ((32, N), (32, N + TAIL), (32, N + TAIL), (32, N + TAIL))
    return pl.pallas_call(
        product_kernel,
        in_specs=[
            pl.BlockSpec(memory_space=pltpu.SMEM),
            pl.BlockSpec(memory_space=pltpu.VMEM),
            pl.BlockSpec(memory_space=pl.ANY),
        ],
        out_shape=[jax.ShapeDtypeStruct(s, F32 if n == 0 else I16) for n, s in enumerate(outs)],
        scratch_shapes=[
            pltpu.VMEM((128, N), F32),
            pltpu.VMEM(w.shape, w.dtype),
            pltpu.SemaphoreType.DMA((TILES,)),
        ],
        compiler_params=pltpu.CompilerParams(vmem_limit_bytes=50 * 2**20),
        cost_estimate=pl.CostEstimate(flops=2 * 128 * 512 * N, bytes_accessed=6 * 2**20, transcendentals=0),
    )(z, x, w)


def pack(ref, values):
    q, k = encode(values)
    ref[:, :HALF] = to_i16(jnp.concatenate([q[:, :HALF], q[:, HALF:]], axis=0))
    ref[:, HALF:] = to_i16(jnp.broadcast_to(jnp.concatenate([k, k], axis=0), (16, TAIL)))


def unpack(ref):
    part = to_f32(ref[:, :HALF]) * scale_of(ref[:, HALF:])
    return jnp.concatenate([part[:8], part[8:]], axis=1)


def first_sum_kernel(own_ref, a_ref, b_ref, c_ref, keep_ref, up_ref, far_ref, down_ref):
    total = own_ref[...]
    for ref in (a_ref, b_ref, c_ref):
        total = total + to_f32(ref[:, :N]) * scale_of(ref[:, N:])
    keep_ref[...] = total[:8]
    up_ref[...] = total[8:16]
    pack(far_ref, total[16:24])
    pack(down_ref, total[24:])


def relay_kernel(up_ref, far_ref, out_ref):
    pack(out_ref, up_ref[...] + unpack(far_ref))


ROWS = jax.ShapeDtypeStruct((8, N), F32)
CODED = jax.ShapeDtypeStruct((16, HALF + TAIL), I16)


def call(kernel, outs, *arrays):
    return pl.pallas_call(
        kernel,
        out_shape=outs,
        compiler_params=pltpu.CompilerParams(vmem_limit_bytes=24 * 2**20),
        cost_estimate=pl.CostEstimate(flops=2**20, bytes_accessed=2**20, transcendentals=0),
    )(*arrays)


def stats_kernel(own_ref, a_ref, b_ref, allowed_ref, logits_ref, stats_ref):
    logits = own_ref[...] + unpack(a_ref) + unpack(b_ref)
    logits_ref[...] = logits
    allowed = allowed_ref[...] > 0.5
    top = jnp.max(jnp.where(allowed, logits, -1e30), axis=1, keepdims=True)
    scaled = jnp.where(allowed, jnp.exp(logits - top), 0.0)
    total = jnp.sum(scaled, axis=1, keepdims=True)
    weighted = jnp.sum(jnp.where(allowed, scaled * logits, 0.0), axis=1, keepdims=True)
    own_lane = lax.broadcasted_iota(jnp.int32, (8, 128), 1) == lax.broadcasted_iota(jnp.int32, (8, 128), 0)
    for n, column in enumerate((top, total, weighted)):
        row = jnp.sum(jnp.where(own_lane, column, 0.0), axis=0, keepdims=True)
        stats_ref[:, :, 128 * n : 128 * n + 128] = jnp.broadcast_to(row[None], (32, 1, 128))


def finish_kernel(logits_ref, allowed_ref, stats_ref, log_probs_ref, entropy_ref):
    top = stats_ref[:, :, :128]
    row_max = jnp.max(top, axis=0)
    factor = jnp.exp(top - row_max[None])
    lane = lax.broadcasted_iota(jnp.int32, (1, 128), 1)
    total = jnp.where(lane < 8, jnp.sum(stats_ref[:, :, 128:256] * factor, axis=0), 1.0)
    weighted = jnp.sum(stats_ref[:, :, 256:] * factor, axis=0)
    log_norm = row_max + jnp.log(total)
    entropy_ref[...] = (log_norm - weighted / total)[:, :8]
    own_lane = lax.broadcasted_iota(jnp.int32, (8, 128), 1) == lax.broadcasted_iota(jnp.int32, (8, 128), 0)
    column = jnp.sum(jnp.where(own_lane, log_norm, 0.0), axis=1, keepdims=True)
    log_probs_ref[0] = jnp.where(allowed_ref[...] > 0.5, logits_ref[...] - column, 0.0)


def spread(array, axis):
    return lax.all_to_all(array, axis, 0, 0)


def shift(array, step):
    rows, columns = lax.axis_size("rows"), lax.axis_size("vocab")
    pairs = [
        (z * columns + v, (z + (step if v % 2 == 0 else -step)) % rows * columns + v)
        for z in range(rows)
        for v in range(columns)
    ]
    return lax.ppermute(array, ("rows", "vocab"), pairs)


def shards(hidden_held, head_weight, state_table, row_states, owner):
    z = (lax.axis_index("rows") + 16 * (lax.axis_index("vocab") & 1)).astype(jnp.int32)[None]
    chunks = hidden_held[0, 0].reshape(16, 8, 4, 128).transpose(0, 2, 1, 3).reshape(32, 16, 128)
    mine = lax.dynamic_index_in_dim(spread(chunks, "vocab"), owner[0], 0, keepdims=True)
    x = spread(jnp.broadcast_to(mine, (32, 16, 128)), "vocab")

    own, up, up2, down = product(z, x, head_weight)
    parts = (shift(up, 1), shift(up2, 2), shift(down, -1))
    own, up, far, down = call(first_sum_kernel, [ROWS, ROWS, CODED, CODED], own, *parts)
    far, down = shift(far, 4), shift(down, -4)
    up = shift(call(relay_kernel, CODED, up, far), 4)

    words = state_table[row_states[0]]
    bits = jnp.right_shift(words[:, :, None], jnp.arange(32, dtype=jnp.int32)) & 1
    allowed = bits.astype(F32).reshape(8, N)

    outs = [ROWS, jax.ShapeDtypeStruct((32, 1, 384), F32)]
    logits, stats = call(stats_kernel, outs, own, down, up, allowed)
    stats = spread(stats, "vocab")
    outs = [jax.ShapeDtypeStruct((1, 8, N), F32), jax.ShapeDtypeStruct((1, 8), F32)]
    return tuple(call(finish_kernel, outs, logits, allowed, stats))


def solution(mesh):
    return jax.shard_map(
        shards,
        mesh=mesh,
        in_specs=(
            P("vocab", None, None, "rows"),
            P("rows", "vocab"),
            P(None, "vocab"),
            P(None, "rows"),
            P(),
        ),
        out_specs=(P(None, "rows", "vocab"), P(None, "rows")),
        check_vma=False,
    )
```

```python
import jax
import jax.numpy as jnp
from jax import lax
from jax.experimental import pallas as pl
from jax.experimental.pallas import tpu as pltpu
from jax.sharding import PartitionSpec as P

N = 4096
HALF = N // 2
TAIL = 128
TILES = 8
WIDE = N // TILES
F32 = jnp.float32
I16 = jnp.int16


def encode(values):
    top = jnp.max(jnp.abs(values), axis=1, keepdims=True)
    k = jnp.ceil(8.0 * jnp.log2(jnp.maximum(top, 1e-30) * (1.0 / 32000.0)))
    return jnp.round(values * jnp.exp2(-0.125 * k)), k


def to_i16(values):
    return values.astype(jnp.int32).astype(I16)


def to_f32(codes):
    return codes.astype(jnp.int32).astype(F32)


def scale_of(codes):
    return jnp.exp2(0.125 * to_f32(codes)[:, :1])


def product_kernel(z_ref, x_ref, w_ref, own_ref, down_ref, up2_ref, up_ref, acc_ref, held_ref, sems):
    def tile(t):
        part = pl.ds(t * WIDE, WIDE)
        return pltpu.make_async_copy(w_ref.at[:, part], held_ref.at[:, part], sems.at[t])

    for t in range(TILES):
        tile(t).start()
    x = x_ref[...].astype(F32).reshape(16, 2, 2, 8, 128)
    x = [x[:, h, t].reshape(128, 128) for h in range(2) for t in range(2)]
    x = jnp.concatenate(x, axis=1).astype(jnp.bfloat16)
    i = lax.broadcasted_iota(jnp.int32, (128, 128), 0)
    source = lax.broadcasted_iota(jnp.int32, (128, 128), 1)
    b = i >> 5
    piece = ((z_ref[0] & 15) + (1 - 2 * (z_ref[0] >> 4)) * (jnp.where(b == 3, -1, b) + 4 * ((i >> 3) & 3))) & 15
    chosen = (source == 8 * piece + (i & 7)).astype(F32).astype(jnp.bfloat16)
    x = jnp.dot(chosen, x, preferred_element_type=F32).astype(jnp.bfloat16)
    for t in range(TILES):
        tile(t).wait()
        acc_ref[:, t * WIDE : (t + 1) * WIDE] = jnp.dot(
            x, held_ref[:, t * WIDE : (t + 1) * WIDE], preferred_element_type=F32
        )
    own_ref[...] = acc_ref[:32]
    for ref, lo in ((up_ref, 32), (up2_ref, 64), (down_ref, 96)):
        q, k = encode(acc_ref[lo : lo + 32])
        ref[:, :N] = to_i16(q)
        ref[:, N:] = to_i16(jnp.broadcast_to(k, (32, TAIL)))


def product(z, x, w):
    outs = ((32, N), (32, N + TAIL), (32, N + TAIL), (32, N + TAIL))
    return pl.pallas_call(
        product_kernel,
        in_specs=[
            pl.BlockSpec(memory_space=pltpu.SMEM),
            pl.BlockSpec(memory_space=pltpu.VMEM),
            pl.BlockSpec(memory_space=pl.ANY),
        ],
        out_shape=[jax.ShapeDtypeStruct(s, F32 if n == 0 else I16) for n, s in enumerate(outs)],
        scratch_shapes=[
            pltpu.VMEM((128, N), F32),
            pltpu.VMEM(w.shape, w.dtype),
            pltpu.SemaphoreType.DMA((TILES,)),
        ],
        compiler_params=pltpu.CompilerParams(vmem_limit_bytes=50 * 2**20),
        cost_estimate=pl.CostEstimate(flops=2 * 128 * 512 * N, bytes_accessed=6 * 2**20, transcendentals=0),
    )(z, x, w)


def pack(ref, values):
    q, k = encode(values)
    ref[:, :HALF] = to_i16(jnp.concatenate([q[:, :HALF], q[:, HALF:]], axis=0))
    ref[:, HALF:] = to_i16(jnp.broadcast_to(jnp.concatenate([k, k], axis=0), (16, TAIL)))


def unpack(ref):
    part = to_f32(ref[:, :HALF]) * scale_of(ref[:, HALF:])
    return jnp.concatenate([part[:8], part[8:]], axis=1)


def first_sum_kernel(own_ref, a_ref, b_ref, c_ref, keep_ref, up_ref, far_ref, down_ref):
    total = own_ref[...]
    for ref in (a_ref, b_ref, c_ref):
        total = total + to_f32(ref[:, :N]) * scale_of(ref[:, N:])
    keep_ref[...] = total[:8]
    up_ref[...] = total[8:16]
    pack(far_ref, total[16:24])
    pack(down_ref, total[24:])


def relay_kernel(up_ref, far_ref, out_ref):
    pack(out_ref, up_ref[...] + unpack(far_ref))


ROWS = jax.ShapeDtypeStruct((8, N), F32)
CODED = jax.ShapeDtypeStruct((16, HALF + TAIL), I16)


def call(kernel, outs, *arrays):
    return pl.pallas_call(
        kernel,
        out_shape=outs,
        compiler_params=pltpu.CompilerParams(vmem_limit_bytes=24 * 2**20),
        cost_estimate=pl.CostEstimate(flops=2**20, bytes_accessed=2**20, transcendentals=0),
    )(*arrays)


def stats_kernel(own_ref, a_ref, b_ref, allowed_ref, logits_ref, stats_ref):
    logits = own_ref[...] + unpack(a_ref) + unpack(b_ref)
    logits_ref[...] = logits
    allowed = allowed_ref[...] > 0.5
    top = jnp.max(jnp.where(allowed, logits, -1e30), axis=1, keepdims=True)
    scaled = jnp.where(allowed, jnp.exp(logits - top), 0.0)
    total = jnp.sum(scaled, axis=1, keepdims=True)
    weighted = jnp.sum(jnp.where(allowed, scaled * logits, 0.0), axis=1, keepdims=True)
    own_lane = lax.broadcasted_iota(jnp.int32, (8, 128), 1) == lax.broadcasted_iota(jnp.int32, (8, 128), 0)
    for n, column in enumerate((top, total, weighted)):
        row = jnp.sum(jnp.where(own_lane, column, 0.0), axis=0, keepdims=True)
        stats_ref[:, :, 128 * n : 128 * n + 128] = jnp.broadcast_to(row[None], (32, 1, 128))


def finish_kernel(logits_ref, allowed_ref, stats_ref, log_probs_ref, entropy_ref):
    top = stats_ref[:, :, :128]
    row_max = jnp.max(top, axis=0)
    factor = jnp.exp(top - row_max[None])
    lane = lax.broadcasted_iota(jnp.int32, (1, 128), 1)
    total = jnp.where(lane < 8, jnp.sum(stats_ref[:, :, 128:256] * factor, axis=0), 1.0)
    weighted = jnp.sum(stats_ref[:, :, 256:] * factor, axis=0)
    log_norm = row_max + jnp.log(total)
    entropy_ref[...] = (log_norm - weighted / total)[:, :8]
    own_lane = lax.broadcasted_iota(jnp.int32, (8, 128), 1) == lax.broadcasted_iota(jnp.int32, (8, 128), 0)
    column = jnp.sum(jnp.where(own_lane, log_norm, 0.0), axis=1, keepdims=True)
    log_probs_ref[0] = jnp.where(allowed_ref[...] > 0.5, logits_ref[...] - column, 0.0)


def spread(array, axis):
    return lax.all_to_all(array, axis, 0, 0)


def shift(array, step):
    rows, columns = lax.axis_size("rows"), lax.axis_size("vocab")
    pairs = [
        (z * columns + v, (z + (step if v % 2 == 0 else -step)) % rows * columns + v)
        for z in range(rows)
        for v in range(columns)
    ]
    return lax.ppermute(array, ("rows", "vocab"), pairs)


def shards(hidden_held, head_weight, state_table, row_states, owner):
    z = (lax.axis_index("rows") + 16 * (lax.axis_index("vocab") & 1)).astype(jnp.int32)[None]
    chunks = hidden_held[0, 0].reshape(16, 8, 4, 128).transpose(0, 2, 1, 3).reshape(32, 16, 128)
    mine = lax.dynamic_index_in_dim(spread(chunks, "vocab"), owner[0], 0, keepdims=True)
    x = spread(jnp.broadcast_to(mine, (32, 16, 128)), "vocab")
    words = state_table[row_states[0]]
    bits = jnp.right_shift(words[:, :, None], jnp.arange(32, dtype=jnp.int32)) & 1
    allowed = bits.astype(F32).reshape(8, N)

    x, allowed = lax.optimization_barrier((x, allowed))

    own, down, up2, up = product(z, x, head_weight)
    parts = (shift(down, -1), shift(up2, 2), shift(up, 1))
    own, up, far, down = call(first_sum_kernel, [ROWS, ROWS, CODED, CODED], own, *parts)
    far, down = shift(far, 4), shift(down, -4)
    up = shift(call(relay_kernel, CODED, up, far), 4)

    outs = [ROWS, jax.ShapeDtypeStruct((32, 1, 384), F32)]
    logits, stats = call(stats_kernel, outs, own, down, up, allowed)
    stats = spread(stats, "vocab")
    outs = [jax.ShapeDtypeStruct((1, 8, N), F32), jax.ShapeDtypeStruct((1, 8), F32)]
    return tuple(call(finish_kernel, outs, logits, allowed, stats))


def solution(mesh):
    return jax.shard_map(
        shards,
        mesh=mesh,
        in_specs=(
            P("vocab", None, None, "rows"),
            P("rows", "vocab"),
            P(None, "vocab"),
            P(None, "rows"),
            P(),
        ),
        out_specs=(P(None, "rows", "vocab"), P(None, "rows")),
        check_vma=False,
    )
```

```python
import jax
import jax.numpy as jnp
from jax import lax
from jax.experimental import pallas as pl
from jax.experimental.pallas import tpu as pltpu
from jax.sharding import PartitionSpec as P

N = 4096
HALF = N // 2
TAIL = 128
TILES = 4
WIDE = N // TILES
AHEAD = 3
F32 = jnp.float32
I16 = jnp.int16


def encode(values):
    top = jnp.max(jnp.abs(values), axis=1, keepdims=True)
    k = jnp.ceil(8.0 * jnp.log2(jnp.maximum(top, 1e-30) * (1.0 / 32000.0)))
    return jnp.round(values * jnp.exp2(-0.125 * k)), k


def to_i16(values):
    return values.astype(jnp.int32).astype(I16)


def to_f32(codes):
    return codes.astype(jnp.int32).astype(F32)


def scale_of(codes):
    return jnp.exp2(0.125 * to_f32(codes)[:, :1])


def part(array, t):
    return array.at[:, pl.ds(t * WIDE, WIDE)]


def stage_kernel(w_ref, *refs):
    copies = [pltpu.make_async_copy(part(w_ref, t), refs[t], refs[-1].at[t]) for t in range(AHEAD)]
    for copy in copies:
        copy.start()
    for copy in copies:
        copy.wait()


def stage(w):
    return pl.pallas_call(
        stage_kernel,
        in_specs=[pl.BlockSpec(memory_space=pl.ANY)],
        out_specs=[pl.BlockSpec(memory_space=pl.ANY)] * AHEAD,
        out_shape=[jax.ShapeDtypeStruct((w.shape[0], WIDE), w.dtype)] * AHEAD,
        scratch_shapes=[pltpu.SemaphoreType.DMA((AHEAD,))],
        compiler_params=pltpu.CompilerParams(vmem_limit_bytes=47 * 2**20),
        cost_estimate=pl.CostEstimate(flops=0, bytes_accessed=2**23, transcendentals=0),
    )(w)


def product_kernel(z_ref, x_ref, w_ref, *refs):
    staged, (own_ref, down_ref, up2_ref, up_ref, acc_ref, held_ref, sems) = refs[:AHEAD], refs[AHEAD:]
    copies = [
        pltpu.make_async_copy(part(w_ref, t), part(held_ref, t - AHEAD), sems.at[t - AHEAD]) for t in range(AHEAD, TILES)
    ]
    for copy in copies:
        copy.start()
    x = x_ref[...].astype(F32).reshape(16, 2, 2, 8, 128)
    x = [x[:, h, t].reshape(128, 128) for h in range(2) for t in range(2)]
    x = jnp.concatenate(x, axis=1).astype(jnp.bfloat16)
    i = lax.broadcasted_iota(jnp.int32, (128, 128), 0)
    source = lax.broadcasted_iota(jnp.int32, (128, 128), 1)
    b = i >> 5
    piece = ((z_ref[0] & 15) + (1 - 2 * (z_ref[0] >> 4)) * (jnp.where(b == 3, -1, b) + 4 * ((i >> 3) & 3))) & 15
    chosen = (source == 8 * piece + (i & 7)).astype(F32).astype(jnp.bfloat16)
    x = jnp.dot(chosen, x, preferred_element_type=F32).astype(jnp.bfloat16)
    for t in range(TILES):
        if t < AHEAD:
            tile = staged[t][...]
        else:
            copies[t - AHEAD].wait()
            tile = held_ref[:, (t - AHEAD) * WIDE : (t - AHEAD + 1) * WIDE]
        acc_ref[:, t * WIDE : (t + 1) * WIDE] = jnp.dot(x, tile, preferred_element_type=F32)
    own_ref[...] = acc_ref[:32]
    for ref, lo in ((up_ref, 32), (up2_ref, 64), (down_ref, 96)):
        q, k = encode(acc_ref[lo : lo + 32])
        ref[:, :N] = to_i16(q)
        ref[:, N:] = to_i16(jnp.broadcast_to(k, (32, TAIL)))


def product(z, x, w):
    outs = ((32, N), (32, N + TAIL), (32, N + TAIL), (32, N + TAIL))
    return pl.pallas_call(
        product_kernel,
        in_specs=[
            pl.BlockSpec(memory_space=pltpu.SMEM),
            pl.BlockSpec(memory_space=pltpu.VMEM),
            pl.BlockSpec(memory_space=pl.ANY),
        ]
        + [pl.BlockSpec(memory_space=pltpu.VMEM)] * AHEAD,
        out_shape=[jax.ShapeDtypeStruct(s, F32 if n == 0 else I16) for n, s in enumerate(outs)],
        scratch_shapes=[
            pltpu.VMEM((128, N), F32),
            pltpu.VMEM((w.shape[0], (TILES - AHEAD) * WIDE), w.dtype),
            pltpu.SemaphoreType.DMA((TILES - AHEAD,)),
        ],
        compiler_params=pltpu.CompilerParams(vmem_limit_bytes=47 * 2**20),
        cost_estimate=pl.CostEstimate(flops=2 * 128 * 512 * N, bytes_accessed=6 * 2**20, transcendentals=0),
    )(z, x, w, *stage(w))


def pack(ref, values):
    q, k = encode(values)
    ref[:, :HALF] = to_i16(jnp.concatenate([q[:, :HALF], q[:, HALF:]], axis=0))
    ref[:, HALF:] = to_i16(jnp.broadcast_to(jnp.concatenate([k, k], axis=0), (16, TAIL)))


def unpack(ref):
    part = to_f32(ref[:, :HALF]) * scale_of(ref[:, HALF:])
    return jnp.concatenate([part[:8], part[8:]], axis=1)


def first_sum_kernel(own_ref, a_ref, b_ref, c_ref, keep_ref, up_ref, far_ref, down_ref):
    total = own_ref[...]
    for ref in (a_ref, b_ref, c_ref):
        total = total + to_f32(ref[:, :N]) * scale_of(ref[:, N:])
    keep_ref[...] = total[:8]
    up_ref[...] = total[8:16]
    pack(far_ref, total[16:24])
    pack(down_ref, total[24:])


def relay_kernel(up_ref, far_ref, out_ref):
    pack(out_ref, up_ref[...] + unpack(far_ref))


ROWS = jax.ShapeDtypeStruct((8, N), F32)
CODED = jax.ShapeDtypeStruct((16, HALF + TAIL), I16)


def call(kernel, outs, *arrays):
    return pl.pallas_call(
        kernel,
        out_shape=outs,
        compiler_params=pltpu.CompilerParams(vmem_limit_bytes=24 * 2**20),
        cost_estimate=pl.CostEstimate(flops=2**20, bytes_accessed=2**20, transcendentals=0),
    )(*arrays)


def stats_kernel(own_ref, a_ref, b_ref, allowed_ref, logits_ref, stats_ref):
    logits = own_ref[...] + unpack(a_ref) + unpack(b_ref)
    logits_ref[...] = logits
    allowed = allowed_ref[...] > 0.5
    top = jnp.max(jnp.where(allowed, logits, -1e30), axis=1, keepdims=True)
    scaled = jnp.where(allowed, jnp.exp(logits - top), 0.0)
    total = jnp.sum(scaled, axis=1, keepdims=True)
    weighted = jnp.sum(jnp.where(allowed, scaled * logits, 0.0), axis=1, keepdims=True)
    own_lane = lax.broadcasted_iota(jnp.int32, (8, 128), 1) == lax.broadcasted_iota(jnp.int32, (8, 128), 0)
    for n, column in enumerate((top, total, weighted)):
        row = jnp.sum(jnp.where(own_lane, column, 0.0), axis=0, keepdims=True)
        stats_ref[:, :, 128 * n : 128 * n + 128] = jnp.broadcast_to(row[None], (32, 1, 128))


def finish_kernel(logits_ref, allowed_ref, stats_ref, log_probs_ref, entropy_ref):
    top = stats_ref[:, :, :128]
    row_max = jnp.max(top, axis=0)
    factor = jnp.exp(top - row_max[None])
    lane = lax.broadcasted_iota(jnp.int32, (1, 128), 1)
    total = jnp.where(lane < 8, jnp.sum(stats_ref[:, :, 128:256] * factor, axis=0), 1.0)
    weighted = jnp.sum(stats_ref[:, :, 256:] * factor, axis=0)
    log_norm = row_max + jnp.log(total)
    entropy_ref[...] = (log_norm - weighted / total)[:, :8]
    own_lane = lax.broadcasted_iota(jnp.int32, (8, 128), 1) == lax.broadcasted_iota(jnp.int32, (8, 128), 0)
    column = jnp.sum(jnp.where(own_lane, log_norm, 0.0), axis=1, keepdims=True)
    log_probs_ref[0] = jnp.where(allowed_ref[...] > 0.5, logits_ref[...] - column, 0.0)


def spread(array, axis):
    return lax.all_to_all(array, axis, 0, 0)


def shift(array, step):
    rows, columns = lax.axis_size("rows"), lax.axis_size("vocab")
    pairs = [
        (z * columns + v, (z + (step if v % 2 == 0 else -step)) % rows * columns + v)
        for z in range(rows)
        for v in range(columns)
    ]
    return lax.ppermute(array, ("rows", "vocab"), pairs)


def shards(hidden_held, head_weight, state_table, row_states, owner):
    z = (lax.axis_index("rows") + 16 * (lax.axis_index("vocab") & 1)).astype(jnp.int32)[None]
    chunks = hidden_held[0, 0].reshape(16, 8, 4, 128).transpose(0, 2, 1, 3).reshape(32, 16, 128)
    mine = lax.dynamic_index_in_dim(spread(chunks, "vocab"), owner[0], 0, keepdims=True)
    x = spread(jnp.broadcast_to(mine, (32, 16, 128)), "vocab")
    words = state_table[row_states[0]]
    bits = jnp.right_shift(words[:, :, None], jnp.arange(32, dtype=jnp.int32)) & 1
    allowed = bits.astype(F32).reshape(8, N)

    x, allowed = lax.optimization_barrier((x, allowed))

    own, down, up2, up = product(z, x, head_weight)
    parts = (shift(down, -1), shift(up2, 2), shift(up, 1))
    own, up, far, down = call(first_sum_kernel, [ROWS, ROWS, CODED, CODED], own, *parts)
    far, down = shift(far, 4), shift(down, -4)
    up = shift(call(relay_kernel, CODED, up, far), 4)

    outs = [ROWS, jax.ShapeDtypeStruct((32, 1, 384), F32)]
    logits, stats = call(stats_kernel, outs, own, down, up, allowed)
    stats = spread(stats, "vocab")
    outs = [jax.ShapeDtypeStruct((1, 8, N), F32), jax.ShapeDtypeStruct((1, 8), F32)]
    return tuple(call(finish_kernel, outs, logits, allowed, stats))


def solution(mesh):
    return jax.shard_map(
        shards,
        mesh=mesh,
        in_specs=(
            P("vocab", None, None, "rows"),
            P("rows", "vocab"),
            P(None, "vocab"),
            P(None, "rows"),
            P(),
        ),
        out_specs=(P(None, "rows", "vocab"), P(None, "rows")),
        check_vma=False,
    )
```

```python
import jax
import jax.numpy as jnp
from jax import lax
from jax.experimental import pallas as pl
from jax.experimental.pallas import tpu as pltpu
from jax.sharding import PartitionSpec as P

N = 4096
HALF = N // 2
TAIL = 128
TILES = 4
WIDE = N // TILES
AHEAD = 3
F32 = jnp.float32
I16 = jnp.int16


def encode(values):
    top = jnp.max(jnp.abs(values), axis=1, keepdims=True)
    k = jnp.ceil(8.0 * jnp.log2(jnp.maximum(top, 1e-30) * (1.0 / 32000.0)))
    return jnp.round(values * jnp.exp2(-0.125 * k)), k


def to_i16(values):
    return values.astype(jnp.int32).astype(I16)


def to_f32(codes):
    return codes.astype(jnp.int32).astype(F32)


def scale_of(codes):
    return jnp.exp2(0.125 * to_f32(codes)[:, :1])


def choose_kernel(owner_ref, chunks_ref, out_ref):
    out_ref[...] = jnp.broadcast_to(chunks_ref[pl.ds(owner_ref[0], 1)], out_ref.shape)


def choose(owner, chunks):
    return pl.pallas_call(
        choose_kernel,
        in_specs=[pl.BlockSpec(memory_space=pltpu.SMEM), pl.BlockSpec(memory_space=pltpu.VMEM)],
        out_shape=jax.ShapeDtypeStruct(chunks.shape, chunks.dtype),
        compiler_params=pltpu.CompilerParams(vmem_limit_bytes=24 * 2**20),
    )(owner, chunks)


def part(array, t):
    return array.at[:, pl.ds(t * WIDE, WIDE)]


def stage_kernel(w_ref, *refs):
    copies = [pltpu.make_async_copy(part(w_ref, t), refs[t], refs[-1].at[t]) for t in range(AHEAD)]
    for copy in copies:
        copy.start()
    for copy in copies:
        copy.wait()


def stage(w):
    return pl.pallas_call(
        stage_kernel,
        in_specs=[pl.BlockSpec(memory_space=pl.ANY)],
        out_specs=[pl.BlockSpec(memory_space=pl.ANY)] * AHEAD,
        out_shape=[jax.ShapeDtypeStruct((w.shape[0], WIDE), w.dtype)] * AHEAD,
        scratch_shapes=[pltpu.SemaphoreType.DMA((AHEAD,))],
        compiler_params=pltpu.CompilerParams(vmem_limit_bytes=47 * 2**20),
        cost_estimate=pl.CostEstimate(flops=0, bytes_accessed=2**23, transcendentals=0),
    )(w)


def product_kernel(z_ref, x_ref, w_ref, *refs):
    staged, (own_ref, down_ref, up2_ref, up_ref, acc_ref, held_ref, sems) = refs[:AHEAD], refs[AHEAD:]
    copies = [
        pltpu.make_async_copy(part(w_ref, t), part(held_ref, t - AHEAD), sems.at[t - AHEAD]) for t in range(AHEAD, TILES)
    ]
    for copy in copies:
        copy.start()
    x = x_ref[...].astype(F32).reshape(16, 2, 2, 8, 128)
    x = [x[:, h, t].reshape(128, 128) for h in range(2) for t in range(2)]
    x = jnp.concatenate(x, axis=1).astype(jnp.bfloat16)
    i = lax.broadcasted_iota(jnp.int32, (128, 128), 0)
    source = lax.broadcasted_iota(jnp.int32, (128, 128), 1)
    b = i >> 5
    piece = ((z_ref[0] & 15) + (1 - 2 * (z_ref[0] >> 4)) * (jnp.where(b == 3, -1, b) + 4 * ((i >> 3) & 3))) & 15
    chosen = (source == 8 * piece + (i & 7)).astype(F32).astype(jnp.bfloat16)
    x = jnp.dot(chosen, x, preferred_element_type=F32).astype(jnp.bfloat16)
    for t in range(TILES):
        if t < AHEAD:
            tile = staged[t][...]
        else:
            copies[t - AHEAD].wait()
            tile = held_ref[:, (t - AHEAD) * WIDE : (t - AHEAD + 1) * WIDE]
        acc_ref[:, t * WIDE : (t + 1) * WIDE] = jnp.dot(x, tile, preferred_element_type=F32)
    own_ref[...] = acc_ref[:32]
    for ref, lo in ((up_ref, 32), (up2_ref, 64), (down_ref, 96)):
        q, k = encode(acc_ref[lo : lo + 32])
        ref[:, :N] = to_i16(q)
        ref[:, N:] = to_i16(jnp.broadcast_to(k, (32, TAIL)))


def product(z, x, w):
    outs = ((32, N), (32, N + TAIL), (32, N + TAIL), (32, N + TAIL))
    return pl.pallas_call(
        product_kernel,
        in_specs=[
            pl.BlockSpec(memory_space=pltpu.SMEM),
            pl.BlockSpec(memory_space=pltpu.VMEM),
            pl.BlockSpec(memory_space=pl.ANY),
        ]
        + [pl.BlockSpec(memory_space=pltpu.VMEM)] * AHEAD,
        out_shape=[jax.ShapeDtypeStruct(s, F32 if n == 0 else I16) for n, s in enumerate(outs)],
        scratch_shapes=[
            pltpu.VMEM((128, N), F32),
            pltpu.VMEM((w.shape[0], (TILES - AHEAD) * WIDE), w.dtype),
            pltpu.SemaphoreType.DMA((TILES - AHEAD,)),
        ],
        compiler_params=pltpu.CompilerParams(vmem_limit_bytes=47 * 2**20),
        cost_estimate=pl.CostEstimate(flops=2 * 128 * 512 * N, bytes_accessed=6 * 2**20, transcendentals=0),
    )(z, x, w, *stage(w))


def pack(ref, values):
    q, k = encode(values)
    ref[:, :HALF] = to_i16(jnp.concatenate([q[:, :HALF], q[:, HALF:]], axis=0))
    ref[:, HALF:] = to_i16(jnp.broadcast_to(jnp.concatenate([k, k], axis=0), (16, TAIL)))


def unpack(ref):
    part = to_f32(ref[:, :HALF]) * scale_of(ref[:, HALF:])
    return jnp.concatenate([part[:8], part[8:]], axis=1)


def first_sum_kernel(own_ref, a_ref, b_ref, c_ref, keep_ref, up_ref, far_ref, down_ref):
    total = own_ref[...]
    for ref in (a_ref, b_ref, c_ref):
        total = total + to_f32(ref[:, :N]) * scale_of(ref[:, N:])
    keep_ref[...] = total[:8]
    up_ref[...] = total[8:16]
    pack(far_ref, total[16:24])
    pack(down_ref, total[24:])


def relay_kernel(up_ref, far_ref, out_ref):
    pack(out_ref, up_ref[...] + unpack(far_ref))


ROWS = jax.ShapeDtypeStruct((8, N), F32)
CODED = jax.ShapeDtypeStruct((16, HALF + TAIL), I16)


def call(kernel, outs, *arrays):
    return pl.pallas_call(
        kernel,
        out_shape=outs,
        compiler_params=pltpu.CompilerParams(vmem_limit_bytes=24 * 2**20),
        cost_estimate=pl.CostEstimate(flops=2**20, bytes_accessed=2**20, transcendentals=0),
    )(*arrays)


def stats_kernel(own_ref, a_ref, b_ref, allowed_ref, logits_ref, stats_ref):
    logits = own_ref[...] + unpack(a_ref) + unpack(b_ref)
    logits_ref[...] = logits
    allowed = allowed_ref[...] > 0.5
    top = jnp.max(jnp.where(allowed, logits, -1e30), axis=1, keepdims=True)
    scaled = jnp.where(allowed, jnp.exp(logits - top), 0.0)
    total = jnp.sum(scaled, axis=1, keepdims=True)
    weighted = jnp.sum(jnp.where(allowed, scaled * logits, 0.0), axis=1, keepdims=True)
    lane = lax.broadcasted_iota(jnp.int32, (8, 128), 1)
    row = lax.broadcasted_iota(jnp.int32, (8, 128), 0)
    tile = jnp.zeros((8, 128), F32)
    for n, column in enumerate((top, total, weighted)):
        tile = jnp.where(lane == row + 8 * n, column, tile)
    stats_ref[...] = jnp.broadcast_to(jnp.sum(tile, axis=0, keepdims=True)[None], stats_ref.shape)


def finish_kernel(logits_ref, allowed_ref, stats_ref, log_probs_ref, entropy_ref):
    lane = lax.broadcasted_iota(jnp.int32, (1, 128), 1)
    top = stats_ref[...]
    row_max = jnp.max(top, axis=0)
    factor = jnp.where(lane < 8, jnp.exp(top - row_max[None]), 0.0)
    total = jnp.where(lane < 8, jnp.sum(pltpu.roll(top, 120, 2) * factor, axis=0), 1.0)
    weighted = jnp.sum(pltpu.roll(top, 112, 2) * factor, axis=0)
    log_norm = row_max + jnp.log(total)
    entropy_ref[...] = (log_norm - weighted / total)[:, :8]
    own_lane = lax.broadcasted_iota(jnp.int32, (8, 128), 1) == lax.broadcasted_iota(jnp.int32, (8, 128), 0)
    column = jnp.sum(jnp.where(own_lane, log_norm, 0.0), axis=1, keepdims=True)
    log_probs_ref[0] = jnp.where(allowed_ref[...] > 0.5, logits_ref[...] - column, 0.0)


def spread(array, axis):
    return lax.all_to_all(array, axis, 0, 0)


def shift(array, step):
    rows, columns = lax.axis_size("rows"), lax.axis_size("vocab")
    pairs = [
        (z * columns + v, (z + (step if v % 2 == 0 else -step)) % rows * columns + v)
        for z in range(rows)
        for v in range(columns)
    ]
    return lax.ppermute(array, ("rows", "vocab"), pairs)


def shards(hidden_held, head_weight, state_table, row_states, owner):
    z = (lax.axis_index("rows") + 16 * (lax.axis_index("vocab") & 1)).astype(jnp.int32)[None]
    chunks = hidden_held[0, 0].reshape(16, 8, 4, 128).transpose(0, 2, 1, 3).reshape(32, 16, 128)
    mine = choose(owner, spread(chunks, "vocab"))
    x = spread(mine, "vocab")
    words = state_table[row_states[0]]
    bits = jnp.right_shift(words[:, :, None], jnp.arange(32, dtype=jnp.int32)) & 1
    allowed = bits.astype(F32).reshape(8, N)

    x, allowed = lax.optimization_barrier((x, allowed))

    own, down, up2, up = product(z, x, head_weight)
    parts = (shift(down, -1), shift(up2, 2), shift(up, 1))
    own, up, far, down = call(first_sum_kernel, [ROWS, ROWS, CODED, CODED], own, *parts)
    far, down = shift(far, 4), shift(down, -4)
    up = shift(call(relay_kernel, CODED, up, far), 4)

    outs = [ROWS, jax.ShapeDtypeStruct((32, 1, 128), F32)]
    logits, stats = call(stats_kernel, outs, own, down, up, allowed)
    stats = spread(stats, "vocab")
    outs = [jax.ShapeDtypeStruct((1, 8, N), F32), jax.ShapeDtypeStruct((1, 8), F32)]
    return tuple(call(finish_kernel, outs, logits, allowed, stats))


def solution(mesh):
    return jax.shard_map(
        shards,
        mesh=mesh,
        in_specs=(
            P("vocab", None, None, "rows"),
            P("rows", "vocab"),
            P(None, "vocab"),
            P(None, "rows"),
            P(),
        ),
        out_specs=(P(None, "rows", "vocab"), P(None, "rows")),
        check_vma=False,
    )
```

```python
import jax
import jax.numpy as jnp
from jax import lax
from jax.experimental import pallas as pl
from jax.experimental.pallas import tpu as pltpu
from jax.sharding import PartitionSpec as P

N = 4096
TAIL = 128
TILES = 4
WIDE = N // TILES
AHEAD = 3
F32 = jnp.float32
I16 = jnp.int16


def encode(values):
    top = jnp.max(jnp.abs(values), axis=1, keepdims=True)
    k = jnp.ceil(8.0 * jnp.log2(jnp.maximum(top, 1e-30) * (1.0 / 32000.0)))
    return jnp.round(values * jnp.exp2(-0.125 * k)), k


def to_i16(values):
    return values.astype(jnp.int32).astype(I16)


def to_f32(codes):
    return codes.astype(jnp.int32).astype(F32)


def scale_of(codes):
    return jnp.exp2(0.125 * to_f32(codes)[:, :1])


def choose_kernel(owner_ref, chunks_ref, out_ref):
    out_ref[...] = jnp.broadcast_to(chunks_ref[pl.ds(owner_ref[0], 1)], out_ref.shape)


def choose(owner, chunks):
    return pl.pallas_call(
        choose_kernel,
        in_specs=[pl.BlockSpec(memory_space=pltpu.SMEM), pl.BlockSpec(memory_space=pltpu.VMEM)],
        out_shape=jax.ShapeDtypeStruct(chunks.shape, chunks.dtype),
        compiler_params=pltpu.CompilerParams(vmem_limit_bytes=24 * 2**20),
    )(owner, chunks)


def part(array, t):
    return array.at[:, pl.ds(t * WIDE, WIDE)]


def stage_kernel(w_ref, *refs):
    copies = [pltpu.make_async_copy(part(w_ref, t), refs[t], refs[-1].at[t]) for t in range(AHEAD)]
    for copy in copies:
        copy.start()
    for copy in copies:
        copy.wait()


def stage(w):
    return pl.pallas_call(
        stage_kernel,
        in_specs=[pl.BlockSpec(memory_space=pl.ANY)],
        out_specs=[pl.BlockSpec(memory_space=pl.ANY)] * AHEAD,
        out_shape=[jax.ShapeDtypeStruct((w.shape[0], WIDE), w.dtype)] * AHEAD,
        scratch_shapes=[pltpu.SemaphoreType.DMA((AHEAD,))],
        compiler_params=pltpu.CompilerParams(vmem_limit_bytes=47 * 2**20),
        cost_estimate=pl.CostEstimate(flops=0, bytes_accessed=2**23, transcendentals=0),
    )(w)


def product_kernel(z_ref, x_ref, w_ref, *refs):
    staged, (own_ref, down_ref, up2_ref, up_ref, acc_ref, held_ref, sems) = refs[:AHEAD], refs[AHEAD:]
    copies = [
        pltpu.make_async_copy(part(w_ref, t), part(held_ref, t - AHEAD), sems.at[t - AHEAD]) for t in range(AHEAD, TILES)
    ]
    for copy in copies:
        copy.start()
    x = x_ref[...].astype(F32).reshape(16, 2, 2, 8, 128)
    x = [x[:, h, t].reshape(128, 128) for h in range(2) for t in range(2)]
    x = jnp.concatenate(x, axis=1).astype(jnp.bfloat16)
    i = lax.broadcasted_iota(jnp.int32, (128, 128), 0)
    source = lax.broadcasted_iota(jnp.int32, (128, 128), 1)
    b = i >> 5
    piece = ((z_ref[0] & 15) + (1 - 2 * (z_ref[0] >> 4)) * (jnp.where(b == 3, -1, b) + 4 * ((i >> 3) & 3))) & 15
    chosen = (source == 8 * piece + (i & 7)).astype(F32).astype(jnp.bfloat16)
    x = jnp.dot(chosen, x, preferred_element_type=F32).astype(jnp.bfloat16)
    for t in range(TILES):
        if t < AHEAD:
            tile = staged[t][...]
        else:
            copies[t - AHEAD].wait()
            tile = held_ref[:, (t - AHEAD) * WIDE : (t - AHEAD + 1) * WIDE]
        acc_ref[:, t * WIDE : (t + 1) * WIDE] = jnp.dot(x, tile, preferred_element_type=F32)
    own_ref[...] = acc_ref[:32]
    for ref, lo in ((up_ref, 32), (up2_ref, 64), (down_ref, 96)):
        q, k = encode(acc_ref[lo : lo + 32])
        ref[:, :N] = to_i16(q)
        ref[:, N:] = to_i16(jnp.broadcast_to(k, (32, TAIL)))


def product(z, x, w):
    outs = ((32, N), (32, N + TAIL), (32, N + TAIL), (32, N + TAIL))
    return pl.pallas_call(
        product_kernel,
        in_specs=[
            pl.BlockSpec(memory_space=pltpu.SMEM),
            pl.BlockSpec(memory_space=pltpu.VMEM),
            pl.BlockSpec(memory_space=pl.ANY),
        ]
        + [pl.BlockSpec(memory_space=pltpu.VMEM)] * AHEAD,
        out_shape=[jax.ShapeDtypeStruct(s, F32 if n == 0 else I16) for n, s in enumerate(outs)],
        scratch_shapes=[
            pltpu.VMEM((128, N), F32),
            pltpu.VMEM((w.shape[0], (TILES - AHEAD) * WIDE), w.dtype),
            pltpu.SemaphoreType.DMA((TILES - AHEAD,)),
        ],
        compiler_params=pltpu.CompilerParams(vmem_limit_bytes=47 * 2**20),
        cost_estimate=pl.CostEstimate(flops=2 * 128 * 512 * N, bytes_accessed=6 * 2**20, transcendentals=0),
    )(z, x, w, *stage(w))


def pack(ref, values):
    q, k = encode(values)
    ref[:, :N] = to_i16(q)
    ref[:, N:] = to_i16(jnp.broadcast_to(k, (8, TAIL)))


def unpack(ref):
    return to_f32(ref[:, :N]) * scale_of(ref[:, N:])


def first_sum_kernel(own_ref, a_ref, b_ref, c_ref, keep_ref, up_ref, far_ref, down_ref):
    total = own_ref[...]
    for ref in (a_ref, b_ref, c_ref):
        total = total + to_f32(ref[:, :N]) * scale_of(ref[:, N:])
    keep_ref[...] = total[:8]
    up_ref[...] = total[8:16]
    pack(far_ref, total[16:24])
    pack(down_ref, total[24:])


def relay_kernel(up_ref, far_ref, out_ref):
    pack(out_ref, up_ref[...] + unpack(far_ref))


ROWS = jax.ShapeDtypeStruct((8, N), F32)
CODED = jax.ShapeDtypeStruct((8, N + TAIL), I16)


def call(kernel, outs, *arrays):
    return pl.pallas_call(
        kernel,
        out_shape=outs,
        compiler_params=pltpu.CompilerParams(vmem_limit_bytes=24 * 2**20),
        cost_estimate=pl.CostEstimate(flops=2**20, bytes_accessed=2**20, transcendentals=0),
    )(*arrays)


def stats_kernel(own_ref, a_ref, b_ref, allowed_ref, logits_ref, stats_ref):
    logits = own_ref[...] + unpack(a_ref) + unpack(b_ref)
    logits_ref[...] = logits
    allowed = allowed_ref[...] > 0.5
    top = jnp.max(jnp.where(allowed, logits, -1e30), axis=1, keepdims=True)
    scaled = jnp.where(allowed, jnp.exp(logits - top), 0.0)
    total = jnp.sum(scaled, axis=1, keepdims=True)
    weighted = jnp.sum(jnp.where(allowed, scaled * logits, 0.0), axis=1, keepdims=True)
    lane = lax.broadcasted_iota(jnp.int32, (8, 128), 1)
    row = lax.broadcasted_iota(jnp.int32, (8, 128), 0)
    tile = jnp.zeros((8, 128), F32)
    for n, column in enumerate((top, total, weighted)):
        tile = jnp.where(lane == row + 8 * n, column, tile)
    stats_ref[...] = jnp.broadcast_to(jnp.sum(tile, axis=0, keepdims=True)[None], stats_ref.shape)


def finish_kernel(logits_ref, allowed_ref, stats_ref, log_probs_ref, entropy_ref):
    lane = lax.broadcasted_iota(jnp.int32, (1, 128), 1)
    top = stats_ref[...]
    row_max = jnp.max(top, axis=0)
    factor = jnp.where(lane < 8, jnp.exp(top - row_max[None]), 0.0)
    total = jnp.where(lane < 8, jnp.sum(pltpu.roll(top, 120, 2) * factor, axis=0), 1.0)
    weighted = jnp.sum(pltpu.roll(top, 112, 2) * factor, axis=0)
    log_norm = row_max + jnp.log(total)
    entropy_ref[...] = (log_norm - weighted / total)[:, :8]
    own_lane = lax.broadcasted_iota(jnp.int32, (8, 128), 1) == lax.broadcasted_iota(jnp.int32, (8, 128), 0)
    column = jnp.sum(jnp.where(own_lane, log_norm, 0.0), axis=1, keepdims=True)
    log_probs_ref[0] = jnp.where(allowed_ref[...] > 0.5, logits_ref[...] - column, 0.0)


def spread(array, axis):
    return lax.all_to_all(array, axis, 0, 0)


def shift(array, step):
    rows, columns = lax.axis_size("rows"), lax.axis_size("vocab")
    pairs = [
        (z * columns + v, (z + (step if v % 2 == 0 else -step)) % rows * columns + v)
        for z in range(rows)
        for v in range(columns)
    ]
    return lax.ppermute(array, ("rows", "vocab"), pairs)


def shards(hidden_held, head_weight, state_table, row_states, owner):
    z = (lax.axis_index("rows") + 16 * (lax.axis_index("vocab") & 1)).astype(jnp.int32)[None]
    chunks = hidden_held[0, 0].reshape(16, 8, 4, 128).transpose(0, 2, 1, 3).reshape(32, 16, 128)
    mine = choose(owner, spread(chunks, "vocab"))
    x = spread(mine, "vocab")
    words = state_table[row_states[0]]
    bits = jnp.right_shift(words[:, :, None], jnp.arange(32, dtype=jnp.int32)) & 1
    allowed = bits.astype(F32).reshape(8, N)

    x, allowed = lax.optimization_barrier((x, allowed))

    own, down, up2, up = product(z, x, head_weight)
    parts = (shift(down, -1), shift(up2, 2), shift(up, 1))
    own, up, far, down = call(first_sum_kernel, [ROWS, ROWS, CODED, CODED], own, *parts)
    far, down = shift(far, 4), shift(down, -4)
    up = shift(call(relay_kernel, CODED, up, far), 4)

    outs = [ROWS, jax.ShapeDtypeStruct((32, 1, 128), F32)]
    logits, stats = call(stats_kernel, outs, own, down, up, allowed)
    stats = spread(stats, "vocab")
    outs = [jax.ShapeDtypeStruct((1, 8, N), F32), jax.ShapeDtypeStruct((1, 8), F32)]
    return tuple(call(finish_kernel, outs, logits, allowed, stats))


def solution(mesh):
    return jax.shard_map(
        shards,
        mesh=mesh,
        in_specs=(
            P("vocab", None, None, "rows"),
            P("rows", "vocab"),
            P(None, "vocab"),
            P(None, "rows"),
            P(),
        ),
        out_specs=(P(None, "rows", "vocab"), P(None, "rows")),
        check_vma=False,
    )
```
